512 devices in a mesh: dp: 4 (over y), vocab: 128 (over z, x, core).
Axes of the slice: x: 4, y: 4, z: 16, core: 2. Of those that a mesh axis runs over, the one named last changes fastest.
Arguments:
- hidden: bfloat16 [768, 5120], P('dp', 'vocab'), may hold values from -128 to 128
- head: bfloat16 [114688, 5120], P('vocab', 'dp'), may hold values from -0.125 to 0.125
- targets: int32 [4, 192], P('dp'), may hold values from 0 to 114687
- segments: int32 [4, 192], P('dp'), may hold values from 0 to 15, never falling along the last dimension, each value on 1 to 32 neighbouring positions
- loss_mask: int32 [4, 192], P('dp'), may hold values 0 or 1
Outputs:
- grad_hidden: bfloat16 [768, 5120], P('dp', 'vocab')
- grad_head: bfloat16 [114688, 5120], P('vocab', 'dp')
The draws below stay inside these ranges and needn't reach their ends.
All inputs are finite; a program needn't handle non-finite values. No bound on the sum of `loss_mask` on one device may be relied on, other than what follows from the above.
Results may differ from the reference program's by a relative error of at most 0.0055.
Values may be sent and summed in bfloat16 or wider, within the bound.
No kernel may reach another device: no remote copies, remote signals or barrier semaphores. Data moves between devices by JAX's collectives and lax.ppermute only.
A program may use at most 64 MiB of HBM per device.

```python
import math
import jax
import jax.numpy as jnp
import numpy as np

D = 5120
TOK = 192
SEGS = 16
MOST = 32
VOCAB = 114688
GROUPS = 4
TOKENS = 768


def draw_rows(key, shape, half):
    return jax.random.uniform(key, shape, jnp.float32, -half, half)


def head_values(key, half):
    return draw_rows(key, (VOCAB, D), half)


def draw_head(key, part):
    shared = head_values(key, 0.125)
    return shared.astype(jnp.bfloat16)


def align_rows(values, shared, keys, half):
    count = min(8, TOKENS // 2)
    picked = jax.random.permutation(keys[2], TOKENS)[:2 * count]
    first = jax.random.randint(keys[3], (count,), 0, VOCAB)
    second = jax.random.randint(keys[4], (count,), 0, VOCAB)
    strength = jnp.array([4.0, 8.0, 12.0, 4.0, 8.0, 12.0, 8.0, 12.0], jnp.float32)[:count]
    factor = strength
    aligned = factor[:, None] * (shared[first] + shared[second])
    fresh = draw_rows(keys[5], (2, count, D), half)
    decoys = factor[:, None] * (fresh[0] + fresh[1])
    values = values.at[picked[:count]].set(aligned)
    return values.at[picked[count:]].set(decoys)


def draw_hidden(key, part):
    half = 0.125
    shared = head_values(key, half)
    key = jax.random.fold_in(key, 7)
    keys = jax.random.split(key, 6)
    values = jnp.clip(jax.random.normal(keys[1], (TOKENS, D), jnp.float32), -4.0, 4.0)
    values = align_rows(values, shared, keys, half)
    return values.astype(jnp.bfloat16)


def plant(drawn, rng, least, high):
    longest = drawn.shape.index(max(drawn.shape))
    spots = []
    for shift in (0, 1):
        where = [jax.random.randint(jax.random.fold_in(rng, axis), (), 0, length) for axis, length in enumerate(drawn.shape)]
        where[longest] = (where[longest] + shift) % drawn.shape[longest]
        spots.append(tuple(where))
    return drawn.at[spots[0]].set(least).at[spots[1]].set(high)


def wide_ids(stream_key, extent, number_of, slope):
    weights = [min(1 << octave, number_of + 1 - (1 << octave)) * (1 << 20) // math.isqrt((1 << octave) ** slope) + 1 for octave in range((number_of + 1).bit_length()) if 1 << octave <= number_of]
    deviation = 1 + sum(weights) // (1 << 30)
    listing = np.cumsum(np.array([max(1, weight // deviation) for weight in weights]))
    ticket = jax.random.randint(jax.random.fold_in(stream_key, 1), extent, 0, int(listing[len(weights) - 1]))
    start = jnp.left_shift(1, jnp.searchsorted(jnp.asarray(listing, jnp.int32), ticket, side="right").astype(jnp.int32))
    rank = start - 1 + jax.random.randint(jax.random.fold_in(stream_key, 4), extent, 0, 1 << 30) % jnp.minimum(start, number_of + 1 - start)
    return jax.random.permutation(jax.random.fold_in(stream_key, 2), number_of)[rank].astype(jnp.int32)


def length_profile(number_of, total, limit, slope):
    loads = [(1 << 20) // math.isqrt(rank ** slope) + 1 for rank in range(2, number_of + 1)]
    surplus, holding = total - limit - (number_of - 1), [1] * (number_of - 1)
    while surplus > 0:
        candidates = [i for i in range(number_of - 1) if holding[i] < limit]
        mass, remaining = sum([loads[i] for i in candidates]), surplus
        for i in candidates:
            extra = min(limit - holding[i], max(1, remaining * loads[i] // mass), surplus)
            holding[i] = holding[i] + extra
            surplus = surplus - extra
    return np.array([limit] + holding)


def uneven(own_key, number_of, total, most, slope):
    if number_of == 2:
        one = jax.random.randint(own_key, (), max(1, total - most), min(most, total - 1) + 1)
        return jnp.stack([one, total - one])
    tallies = jnp.asarray(length_profile(number_of, total, most, slope), jnp.int32)
    pairs = (number_of - 1) // 2
    giver, sink = tallies[1:1 + 2 * pairs:2], tallies[2:2 + 2 * pairs:2]
    slack = jnp.minimum(giver - 1, most - sink)
    moved = jax.random.randint(jax.random.fold_in(own_key, 1), (pairs,), 0, 1 << 20) % (slack + 1)
    tallies = tallies.at[1:1 + 2 * pairs:2].set(giver - moved).at[2:2 + 2 * pairs:2].set(sink + moved)
    return tallies[jax.random.permutation(jax.random.fold_in(own_key, 2), number_of)]


def setup_inputs(seed: int = 0) -> dict:
    arg_keys = jax.random.split(jax.random.key(seed), 6)
    return {
        "hidden": draw_hidden(jax.random.fold_in(arg_keys[5], 71), 0),
        "head": draw_head(jax.random.fold_in(arg_keys[5], 71), 0),
        "targets": plant(wide_ids(arg_keys[2], (GROUPS, TOK), VOCAB, 2), jax.random.fold_in(arg_keys[2], 3), 0, VOCAB - 1).astype(jnp.int32),
        "segments": jax.vmap(lambda own: jnp.searchsorted(jnp.cumsum(uneven(own, SEGS, TOK, MOST, 2)), jnp.arange(TOK), side="right"))(jax.random.split(arg_keys[3], GROUPS)).reshape((GROUPS, TOK)).astype(jnp.int32),
        "loss_mask": plant((jax.random.randint(arg_keys[4], (GROUPS, TOK), 0, 4) < 3).astype(jnp.int32), jax.random.fold_in(arg_keys[4], 1), 0, 1),
    }


loss_scale = 256.0


def reference(hidden, head, targets, segments, loss_mask):
    logits = jnp.dot(hidden, head.T, preferred_element_type=jnp.float32)
    row_max = jnp.max(logits, axis=1, keepdims=True)
    log_norm = row_max + jnp.log(jnp.sum(jnp.exp(logits - row_max), axis=1, keepdims=True))
    mask_f = loss_mask.astype(jnp.float32)
    same = (segments[:, :, None] == segments[:, None, :]).astype(jnp.float32)
    counts = jnp.einsum("gij,gj->gi", same, mask_f)
    weight = (loss_scale * mask_f / jnp.maximum(counts, 1.0)).reshape(-1)
    columns = jnp.arange(VOCAB, dtype=jnp.int32)
    onehot = (targets.reshape(-1)[:, None] == columns[None, :]).astype(jnp.float32)
    grad_logits = (weight[:, None] * (jnp.exp(logits - log_norm) - onehot)).astype(jnp.bfloat16)
    grad_hidden = jnp.dot(grad_logits, head, preferred_element_type=jnp.float32).astype(jnp.bfloat16)
    grad_head = jnp.dot(grad_logits.T, hidden, preferred_element_type=jnp.float32).astype(jnp.bfloat16)
    return grad_hidden, grad_head
```

```python
import jax
import jax.numpy as jnp
from jax import lax
from jax.sharding import Mesh
from jax.sharding import PartitionSpec as P

loss_scale = 256.0
BINS = 4
Z = ("zh", "zl")
f32, bf16 = jnp.float32, jnp.bfloat16


def shift(a, k):
    return lax.ppermute(a, "y", [(i, (i + k) % BINS) for i in range(BINS)])


def swap_core(a):
    return lax.ppermute(a, "c", [(0, 1), (1, 0)])


def swap_pairs():
    return [
        (i * 128 + k * 32 + r, k * 128 + (i - k) % 4 * 32 + r)
        for i in range(4)
        for k in range(4)
        for r in range(32)
    ]


EVERY = ("y", "zh", "zl", "x", "c")


def gather_hidden(hidden):
    tok, cols = hidden.shape
    piece = lax.ppermute(hidden.T, EVERY, swap_pairs())
    along_z = lax.all_to_all(
        jnp.broadcast_to(piece[None], (16, cols, tok)), Z, 0, 0, tiled=True
    )
    along_x = lax.all_to_all(
        jnp.broadcast_to(along_z[None], (4, 16, cols, tok)), "x", 0, 0, tiled=True
    )
    other = swap_core(along_x)
    first = lax.axis_index("c") == 0
    both = jnp.stack([jnp.where(first, along_x, other), jnp.where(first, other, along_x)])
    both = both.reshape(2, 4, BINS, 4, cols, tok)
    return both.transpose(2, 3, 1, 0, 4, 5).reshape(BINS, 32 * cols, tok)


def scatter_hidden(terms, tok, cols):
    parts = terms.astype(bf16).reshape(4, 4, 2, cols, BINS * tok)
    parts = lax.all_to_all(parts.transpose(2, 0, 1, 3, 4), "c", 0, 0, tiled=True)
    parts = jnp.sum(parts.astype(f32), axis=0).astype(bf16)
    parts = lax.all_to_all(parts.transpose(1, 0, 2, 3), "x", 0, 0, tiled=True)
    parts = jnp.sum(parts.astype(f32), axis=0).astype(bf16)
    parts = parts.reshape(4, cols, BINS, tok).transpose(2, 0, 1, 3).reshape(16, cols, tok)
    parts = lax.all_to_all(parts, Z, 0, 0, tiled=True)
    piece = jnp.sum(parts.astype(f32), axis=0).astype(bf16)
    back = lax.ppermute(piece, EVERY, [(b, a) for a, b in swap_pairs()])
    return back.T


def row_stats(local_max, local_sum):
    both = jnp.stack([local_max, local_sum])
    other = swap_core(both)
    top = jnp.maximum(both[0], other[0])
    total = both[1] * jnp.exp(both[0] - top) + other[1] * jnp.exp(other[0] - top)
    both = jnp.stack([top, total])
    every = lax.all_to_all(
        jnp.broadcast_to(both[None], (64,) + both.shape), ("zh", "zl", "x"), 0, 0, tiled=True
    )
    top = jnp.max(every[:, 0], axis=0)
    total = jnp.sum(every[:, 1] * jnp.exp(every[:, 0] - top[None]), axis=0)
    return top + jnp.log(total)


def body(hidden, head, targets, segments, loss_mask):
    tok, cols = hidden.shape
    vocab_rows = head.shape[0]
    half = tok // 2
    features = gather_hidden(hidden)

    def partial_logits(b):
        return lax.dot_general(
            features[b], head, (((0,), (1,)), ((), ())), preferred_element_type=f32
        )

    far = partial_logits(2)
    from_left = shift(far[:half], 1)
    from_right = shift(far[half:], 3)
    up = partial_logits(1)
    down = partial_logits(3)
    up_late = shift(up[half:], 1)
    down_early = shift(down[:half], 3)
    own = partial_logits(0)
    up_early = shift(up[:half] + from_left, 1)
    down_late = shift(down[half:] + from_right, 3)
    logits = own + jnp.concatenate([up_early + down_early, up_late + down_late])

    local_max = jnp.max(logits, axis=1)
    local_sum = jnp.sum(jnp.exp(logits - local_max[:, None]), axis=1)
    log_norm = row_stats(local_max, local_sum)
    mask_f = loss_mask[0].astype(f32)
    seg_ids = segments[0]
    same = (seg_ids[:, None] == seg_ids[None, :]).astype(f32)
    counts = jnp.sum(same * mask_f[None, :], axis=1)
    weight = loss_scale * mask_f / jnp.maximum(counts, 1.0)
    shard = ((lax.axis_index("zh") * 4 + lax.axis_index("zl")) * 4 + lax.axis_index("x")) * 2
    vocab_start = (shard + lax.axis_index("c")) * vocab_rows
    columns = vocab_start + lax.broadcasted_iota(jnp.int32, (1, vocab_rows), 1)
    onehot = (targets[0][:, None] == columns).astype(f32)
    grad_own = (weight[:, None] * (jnp.exp(logits - log_norm[:, None]) - onehot)).astype(bf16)

    grad_down = shift(grad_own, 1)
    grad_up = shift(grad_own, 3)
    far_a = shift(grad_down[:half], 1)
    far_b = shift(grad_up[half:], 3)
    grads = jnp.concatenate([grad_own, grad_up, far_a, far_b, grad_down])

    terms = lax.dot_general(head, grads, (((0,), (1,)), ((), ())), preferred_element_type=f32)
    grad_hidden = scatter_hidden(terms, tok, cols)
    grad_head = sum(
        lax.dot_general(
            grads[b * tok : (b + 1) * tok],
            features[b],
            (((0,), (1,)), ((), ())),
            preferred_element_type=f32,
        )
        for b in range(BINS)
    ).astype(bf16)
    return (grad_hidden, grad_head)


def solution(mesh):
    fine = Mesh(mesh.devices.reshape(4, 4, 4, 4, 2), EVERY)
    row = ("zh", "zl", "x", "c")
    placed = (P("y", row), P(row, "y"), P("y", None), P("y", None), P("y", None))
    return jax.shard_map(
        body,
        mesh=fine,
        in_specs=placed,
        out_specs=(P("y", row), P(row, "y")),
        check_vma=False,
    )
```

```python
import jax
import jax.numpy as jnp
from jax import lax
from jax.sharding import Mesh
from jax.sharding import PartitionSpec as P

loss_scale = 256.0
BINS = 4
EVERY = ("y", "zh", "zl", "x", "c")
ROW = ("zh", "zl", "x", "c")
Z = ("zh", "zl")
f32, bf16 = jnp.float32, jnp.bfloat16


def shift(a, k):
    return lax.ppermute(a, "y", [(i, (i + k) % BINS) for i in range(BINS)])


def swap_core(a):
    return lax.ppermute(a, "c", [(0, 1), (1, 0)])


def exchange(a, axes):
    return lax.all_to_all(a, axes, 0, 0, tiled=True)


def spread(a, axes, n):
    return exchange(jnp.broadcast_to(a[None], (n,) + a.shape), axes)


def column_order(width, cols):
    half = width // 2
    p = lax.broadcasted_iota(jnp.int32, (width, 1), 0)
    core = lax.rem(lax.axis_index("c") + p // half, 2)
    q = lax.rem(p, half)
    natural = lax.rem(q // cols, 4) * (8 * cols) + q // (4 * cols) * (2 * cols) + core * cols + lax.rem(q, cols)
    return (natural == lax.broadcasted_iota(jnp.int32, (1, width), 1)).astype(bf16)


def dot(a, b, ca, cb):
    return lax.dot_general(a, b, (((ca,), (cb,)), ((), ())), preferred_element_type=f32)


def body(hidden, head, targets, segments, loss_mask):
    tok, cols = hidden.shape
    vocab_rows, width = head.shape
    half, hw = tok // 2, width // 2
    y = lax.axis_index("y")
    at = [lax.rem(y + r, BINS) for r in range(BINS)]

    along_z = spread(hidden.T, Z, 16).reshape(BINS, 1, 4 * cols, tok)
    order = column_order(width, cols)
    head_t = dot(order, head, 1, 1).astype(bf16)
    own_cols = exchange(
        jnp.broadcast_to(along_z, (BINS, 4, 4 * cols, tok)).reshape(16, 4 * cols, tok), ("y", "x")
    ).reshape(BINS, hw, tok)
    other_cols = swap_core(own_cols)

    def pick(a, r):
        return lax.dynamic_index_in_dim(a, at[r], 0, keepdims=False)

    def partial_logits(r):
        return dot(pick(own_cols, r), head_t[:hw], 0, 0) + dot(pick(other_cols, r), head_t[hw:], 0, 0)

    far = partial_logits(2)
    from_left = shift(far[:half], 1)
    from_right = shift(far[half:], 3)
    up = partial_logits(1)
    down = partial_logits(3)
    own = partial_logits(0)
    nothing = jnp.zeros((half, vocab_rows), f32)
    up = shift(up + jnp.concatenate([from_left, nothing]), 1)
    down = shift(down + jnp.concatenate([nothing, from_right]), 3)
    logits = own + up + down

    features = jnp.concatenate(
        [
            (dot(pick(own_cols, r), order[:hw], 0, 0) + dot(pick(other_cols, r), order[hw:], 0, 0)).astype(bf16)
            for r in range(BINS)
        ]
    )

    mask_f = loss_mask[0].astype(f32)
    seg_ids = segments[0]
    same = (seg_ids[:, None] == seg_ids[None, :]).astype(f32)
    counts = jnp.sum(same * mask_f[None, :], axis=1)
    weight = loss_scale * mask_f / jnp.maximum(counts, 1.0)
    shard = ((lax.axis_index("zh") * 4 + lax.axis_index("zl")) * 4 + lax.axis_index("x")) * 2
    vocab_start = (shard + lax.axis_index("c")) * vocab_rows
    places = lax.broadcasted_iota(jnp.int32, (1, vocab_rows), 1)
    target = targets[0]

    local_max = jnp.max(logits, axis=1)
    shifted = jnp.exp(logits - local_max[:, None])
    local_lse = local_max + jnp.log(jnp.sum(shifted, axis=1))
    at_target = jnp.sum(jnp.where((target - vocab_start)[:, None] == places, logits, 0.0), axis=1)
    exps = shifted.astype(bf16)

    exps_down = shift(exps, 1)
    exps_up = shift(exps, 3)

    facts = jnp.stack([local_lse, local_max, at_target, weight, target.astype(f32)])
    facts = spread(facts, ("y", "x", "c"), 32).reshape(BINS, 8, 5, tok)
    lse = facts[:, :, 0]
    top = jnp.max(lse, axis=1)
    lse = top + jnp.log(jnp.sum(jnp.exp(lse - top[:, None]), axis=1))
    lse = spread(lse, Z, 16)
    top = jnp.max(lse, axis=0)
    log_norm = top + jnp.log(jnp.sum(jnp.exp(lse - top[None]), axis=0))
    mine = lax.dynamic_index_in_dim(facts, lax.axis_index("x") * 2 + lax.axis_index("c"), 1, keepdims=False)
    scale = mine[:, 3] * jnp.exp(mine[:, 1] - log_norm)
    hit = mine[:, 3] * (jnp.exp(mine[:, 2] - log_norm) - 1.0)
    place = mine[:, 4].astype(jnp.int32) - vocab_start

    far_a = shift(exps_down[:half], 1)
    far_b = shift(exps_up[half:], 3)
    exps_far = jnp.concatenate([far_a, far_b])

    def grad(e, r):
        s, h, p = pick(scale, r), pick(hit, r), pick(place, r)
        return jnp.where(p[:, None] == places, h[:, None], e.astype(f32) * s[:, None]).astype(bf16)

    grads = [grad(e, r) for r, e in enumerate([exps, exps_up, exps_far, exps_down])]

    kept = jnp.zeros((BINS, hw, tok), f32)
    sent = jnp.zeros((BINS, hw, tok), bf16)
    for r in range(BINS):
        kept = lax.dynamic_update_index_in_dim(kept, dot(head_t[:hw], grads[r], 1, 1), at[r], 0)
        sent = lax.dynamic_update_index_in_dim(sent, dot(head_t[hw:], grads[r], 1, 1).astype(bf16), at[r], 0)
    terms = (kept + swap_core(sent).astype(f32)).astype(bf16).reshape(16, 4 * cols, tok)
    terms = exchange(terms, ("y", "x")).reshape(BINS, 4, 4 * cols, tok)
    terms = jnp.sum(terms.astype(f32), axis=1).astype(bf16).reshape(16, cols, tok)
    terms = exchange(terms, Z)
    grad_hidden = jnp.sum(terms.astype(f32), axis=0).astype(bf16).T

    grad_head = dot(jnp.concatenate(grads), features, 0, 0).astype(bf16)
    return (grad_hidden, grad_head)


def solution(mesh):
    fine = Mesh(mesh.devices.reshape(4, 4, 4, 4, 2), EVERY)
    placed = (P("y", ROW), P(ROW, "y"), P("y", None), P("y", None), P("y", None))
    return jax.shard_map(
        body,
        mesh=fine,
        in_specs=placed,
        out_specs=(P("y", ROW), P(ROW, "y")),
        check_vma=False,
    )
```

```python
import functools

import jax
import jax.numpy as jnp
from jax import lax
from jax.experimental import pallas as pl
from jax.experimental.pallas import tpu as pltpu
from jax.sharding import Mesh
from jax.sharding import PartitionSpec as P

loss_scale = 256.0
BINS = 4
EVERY = ("y", "zh", "zl", "x", "c")
ROW = ("zh", "zl", "x", "c")
Z = ("zh", "zl")
COLS, TOK, HIGH, EXTRA = 40, 192, 64, 24
f32, bf16, i32 = jnp.float32, jnp.bfloat16, jnp.int32
VMEM = pl.BlockSpec(memory_space=pltpu.VMEM)
SMEM = pl.BlockSpec(memory_space=pltpu.SMEM)


def shift(a, k):
    return lax.ppermute(a, "y", [(i, (i + k) % BINS) for i in range(BINS)])


def swap_core(a):
    return lax.ppermute(a, "c", [(0, 1), (1, 0)])


def exchange(a, axes):
    return lax.all_to_all(a, axes, 0, 0, tiled=True)


def call(kernel, out, ins, *args, flops=0, nbytes=0):
    return pl.pallas_call(
        kernel,
        out_shape=out,
        in_specs=ins,
        out_specs=[VMEM] * len(out) if isinstance(out, (list, tuple)) else VMEM,
        compiler_params=pltpu.CompilerParams(vmem_limit_bytes=48 * 2**20),
        cost_estimate=pl.CostEstimate(flops=flops, bytes_accessed=nbytes, transcendentals=0),
    )(*args)


def shape(*dims, dtype=f32):
    return jax.ShapeDtypeStruct(dims, dtype)


def packed(piece):
    tail = piece[:, 128:]
    right = jnp.concatenate([tail[EXTRA:], jnp.zeros((2 * EXTRA - COLS, TOK - 128), f32)], axis=0)
    return jnp.concatenate([piece[:, :128], jnp.concatenate([tail[:EXTRA], right], axis=1)], axis=0)


def unpacked(piece):
    tail = jnp.concatenate([piece[COLS:, :64], piece[COLS : 2 * COLS - EXTRA, 64:]], axis=0)
    return jnp.concatenate([piece[:COLS], tail], axis=1)


def pack_kernel(h_ref, o_ref):
    piece = packed(h_ref[...].astype(f32)).astype(bf16)
    for k in range(16):
        o_ref[k] = piece


def unpack_kernel(a_ref, o_ref):
    def one(b, _):
        for p in range(8):
            pair = [unpacked(a_ref[b, 2 * p + k].astype(f32)) for k in range(2)]
            o_ref[b, 2 * COLS * p : 2 * COLS * (p + 1), :] = jnp.concatenate(pair, axis=0).astype(bf16)
        return 0

    lax.fori_loop(0, BINS, one, 0)


def eye():
    return lax.broadcasted_iota(i32, (TOK, TOK), 0) == lax.broadcasted_iota(i32, (TOK, TOK), 1)


def softmax_kernel(own_ref, up_ref, down_ref, place_ref, rows_ref, exps_ref, facts_ref):
    logits = own_ref[...] + up_ref[...] + down_ref[...]
    top = jnp.max(logits, axis=1, keepdims=True)
    shifted = jnp.exp(logits - top)
    lse = top + jnp.log(jnp.sum(shifted, axis=1, keepdims=True))
    places = lax.broadcasted_iota(i32, logits.shape, 1)
    at_target = jnp.sum(jnp.where(place_ref[...] == places, logits, 0.0), axis=1, keepdims=True)
    exps = shifted.astype(bf16)
    for b in range(BINS):
        exps_ref[b] = exps
    same = eye()
    lanes = [jnp.sum(jnp.where(same, v, 0.0), axis=0, keepdims=True) for v in (lse, top, at_target)]
    facts = jnp.concatenate(lanes + [rows_ref[...], jnp.zeros((3, TOK), f32)], axis=0)
    for k in range(32):
        facts_ref[k] = facts


def combine_kernel(facts_ref, o_ref):
    rows = []
    for b in range(BINS):
        part = jnp.concatenate([facts_ref[8 * b + k][0:1] for k in range(8)], axis=0)
        top = jnp.max(part, axis=0, keepdims=True)
        rows.append(top + jnp.log(jnp.sum(jnp.exp(part - top), axis=0, keepdims=True)))
    rows = jnp.concatenate(rows, axis=0)
    for k in range(16):
        o_ref[k] = rows


def grad_kernel(where_ref, lse_ref, facts_ref, exps_ref, head_ref, grads_ref, kept_ref, sent_ref):
    lse = lse_ref[...]
    top = jnp.max(lse, axis=0)
    log_norm = top + jnp.log(jnp.sum(jnp.exp(lse - top[None]), axis=0))
    same = eye()

    def column(row):
        return jnp.sum(jnp.where(same, row, 0.0), axis=1, keepdims=True)

    places = lax.broadcasted_iota(i32, exps_ref.shape[1:], 1) + where_ref[1]
    for b in range(BINS):
        mine = facts_ref[8 * b + where_ref[0]]
        norm = log_norm[b : b + 1]
        scale = column(mine[3:4] * jnp.exp(mine[1:2] - norm))
        hit = column(mine[3:4] * (jnp.exp(mine[2:3] - norm) - 1.0))
        target = column(mine[4:5]).astype(i32)
        grads = jnp.where(target == places, hit, exps_ref[b].astype(f32) * scale).astype(bf16)
        grads_ref[b] = grads
        half = head_ref.shape[0] // 2
        for h, ref in ((1, sent_ref), (0, kept_ref)):
            terms = lax.dot_general(
                head_ref[h * half : (h + 1) * half],
                grads,
                (((1,), (1,)), ((), ())),
                preferred_element_type=f32,
            )
            for p in range(16):
                ref[b, p] = packed(terms[COLS * p : COLS * (p + 1)]).astype(ref.dtype)


def column_order(width):
    half = width // 2
    p = lax.broadcasted_iota(i32, (width, 1), 0)
    core = lax.rem(lax.axis_index("c") + p // half, 2)
    q = lax.rem(p, half)
    natural = lax.rem(q // COLS, 4) * (8 * COLS) + q // (4 * COLS) * (2 * COLS) + core * COLS + lax.rem(q, COLS)
    return (natural == lax.broadcasted_iota(i32, (1, width), 1)).astype(bf16)


def dot(a, b, ca, cb):
    return lax.dot_general(a, b, (((ca,), (cb,)), ((), ())), preferred_element_type=f32)


def body(hidden, head, targets, segments, loss_mask):
    vocab_rows, width = head.shape
    half, hw = TOK // 2, width // 2
    y = lax.axis_index("y")
    at = [lax.rem(y + r, BINS) for r in range(BINS)]

    spread = call(pack_kernel, shape(16, 64, 128, dtype=bf16), [VMEM], hidden.T)
    along_z = exchange(spread, Z).reshape(BINS, 1, 4, 64, 128)
    own_packed = exchange(
        jnp.broadcast_to(along_z, (BINS, 4, 4, 64, 128)).reshape(16, 4, 64, 128), ("y", "x")
    ).reshape(BINS, 16, 64, 128)
    other_packed = swap_core(own_packed)
    order = column_order(width)
    head_t = dot(order, head, 1, 1).astype(bf16)
    unpack = functools.partial(
        call, unpack_kernel, shape(BINS, hw, TOK, dtype=bf16), [VMEM], nbytes=4 * 2**20
    )
    own_cols = unpack(own_packed)
    own_cols, head_t, other_packed = lax.optimization_barrier((own_cols, head_t, other_packed))
    other_cols = unpack(other_packed)

    def pick(a, b):
        return lax.dynamic_index_in_dim(a, b, 0, keepdims=False)

    def partial_logits(r):
        return dot(pick(own_cols, at[r]), head_t[:hw], 0, 0) + dot(pick(other_cols, at[r]), head_t[hw:], 0, 0)

    far = partial_logits(2)
    from_left = shift(far[:half], 1)
    from_right = shift(far[half:], 3)
    up = partial_logits(1)
    down = partial_logits(3)
    own = partial_logits(0)
    nothing = jnp.zeros((half, vocab_rows), f32)
    up = shift(up + jnp.concatenate([from_left, nothing]), 1)
    down = shift(down + jnp.concatenate([nothing, from_right]), 3)

    features = jnp.concatenate(
        [
            (dot(own_cols[b], order[:hw], 0, 0) + dot(other_cols[b], order[hw:], 0, 0)).astype(bf16)
            for b in range(BINS)
        ]
    )

    mask_f = loss_mask[0].astype(f32)
    seg_ids = segments[0]
    same = (seg_ids[:, None] == seg_ids[None, :]).astype(f32)
    counts = jnp.sum(same * mask_f[None, :], axis=1)
    weight = loss_scale * mask_f / jnp.maximum(counts, 1.0)
    shard = ((lax.axis_index("zh") * 4 + lax.axis_index("zl")) * 4 + lax.axis_index("x")) * 2
    vocab_start = (shard + lax.axis_index("c")) * vocab_rows
    place = (targets[0] - vocab_start)[:, None]
    rows = jnp.stack([weight, targets[0].astype(f32)])
    here = jnp.stack([lax.axis_index("x") * 2 + lax.axis_index("c"), vocab_start]).astype(i32)
    up, down, own, features, place, rows = lax.optimization_barrier((up, down, own, features, place, rows))

    exps, facts = call(
        softmax_kernel,
        [shape(BINS, TOK, vocab_rows, dtype=bf16), shape(32, 8, TOK)],
        [VMEM] * 5,
        own,
        up,
        down,
        place,
        rows,
    )
    facts = exchange(facts, ("y", "x", "c"))
    lse = exchange(call(combine_kernel, shape(16, BINS, TOK), [VMEM], facts), Z)
    exps = exchange(exps, "y")

    grads, kept, sent = call(
        grad_kernel,
        [
            shape(BINS, TOK, vocab_rows, dtype=bf16),
            shape(BINS, 16, 64, 128),
            shape(BINS, 16, 64, 128, dtype=bf16),
        ],
        [SMEM] + [VMEM] * 4,
        here,
        lse,
        facts,
        exps,
        head_t,
    )
    terms = swap_core(sent)
    grad_head = dot(grads.reshape(BINS * TOK, vocab_rows), features, 0, 0).astype(bf16)
    terms, grad_head = lax.optimization_barrier((terms, grad_head))
    terms = (kept + terms.astype(f32)).astype(bf16).reshape(16, 4, 64, 128)
    terms = exchange(terms, ("y", "x")).reshape(BINS, 4, 4, 64, 128)
    terms = jnp.sum(terms.astype(f32), axis=1).astype(bf16).reshape(16, 64, 128)
    terms = exchange(terms, Z)
    grad_hidden = unpacked(jnp.sum(terms.astype(f32), axis=0)).astype(bf16).T
    return (grad_hidden, grad_head)


def solution(mesh):
    fine = Mesh(mesh.devices.reshape(4, 4, 4, 4, 2), EVERY)
    placed = (P("y", ROW), P(ROW, "y"), P("y", None), P("y", None), P("y", None))
    return jax.shard_map(
        body,
        mesh=fine,
        in_specs=placed,
        out_specs=(P("y", ROW), P(ROW, "y")),
        check_vma=False,
    )
```

```python
import functools

import jax
import jax.numpy as jnp
from jax import lax
from jax.experimental import pallas as pl
from jax.experimental.pallas import tpu as pltpu
from jax.sharding import Mesh
from jax.sharding import PartitionSpec as P

loss_scale = 256.0
BINS = 4
EVERY = ("y", "zh", "zl", "x", "c")
ROW = ("zh", "zl", "x", "c")
Z = ("zh", "zl")
COLS, TOK, HIGH, EXTRA = 40, 192, 64, 24
f32, bf16, i32 = jnp.float32, jnp.bfloat16, jnp.int32
VMEM = pl.BlockSpec(memory_space=pltpu.VMEM)
SMEM = pl.BlockSpec(memory_space=pltpu.SMEM)


def shift(a, k):
    return lax.ppermute(a, "y", [(i, (i + k) % BINS) for i in range(BINS)])


def swap_core(a):
    return lax.ppermute(a, "c", [(0, 1), (1, 0)])


def exchange(a, axes):
    return lax.all_to_all(a, axes, 0, 0, tiled=True)


def call(kernel, out, ins, *args, flops=0, nbytes=0, scratch=()):
    return pl.pallas_call(
        kernel,
        out_shape=out,
        in_specs=ins,
        scratch_shapes=list(scratch),
        out_specs=[VMEM] * len(out) if isinstance(out, (list, tuple)) else VMEM,
        compiler_params=pltpu.CompilerParams(vmem_limit_bytes=16 * 2**20),
        cost_estimate=pl.CostEstimate(flops=flops, bytes_accessed=nbytes, transcendentals=0),
    )(*args)


def shape(*dims, dtype=f32):
    return jax.ShapeDtypeStruct(dims, dtype)


def packed(piece):
    tail = piece[:, 128:]
    right = jnp.concatenate([tail[EXTRA:], jnp.zeros((2 * EXTRA - COLS, TOK - 128), f32)], axis=0)
    return jnp.concatenate([piece[:, :128], jnp.concatenate([tail[:EXTRA], right], axis=1)], axis=0)


def unpacked(piece):
    tail = jnp.concatenate([piece[COLS:, :64], piece[COLS : 2 * COLS - EXTRA, 64:]], axis=0)
    return jnp.concatenate([piece[:COLS], tail], axis=1)


def pack_kernel(h_ref, o_ref):
    piece = packed(h_ref[...].astype(f32)).astype(bf16)
    for k in range(16):
        o_ref[k] = piece


def unpack_kernel(a_ref, o_ref):
    def one(b, _):
        for p in range(8):
            pair = [unpacked(a_ref[b, 2 * p + k].astype(f32)) for k in range(2)]
            o_ref[b, 2 * COLS * p : 2 * COLS * (p + 1), :] = jnp.concatenate(pair, axis=0).astype(bf16)
        return 0

    lax.fori_loop(0, BINS, one, 0)


def eye():
    return lax.broadcasted_iota(i32, (TOK, TOK), 0) == lax.broadcasted_iota(i32, (TOK, TOK), 1)


def softmax_kernel(logits_ref, place_ref, rows_ref, exps_ref, facts_ref):
    logits = logits_ref[...]
    top = jnp.max(logits, axis=1, keepdims=True)
    shifted = jnp.exp(logits - top)
    lse = top + jnp.log(jnp.sum(shifted, axis=1, keepdims=True))
    places = lax.broadcasted_iota(i32, logits.shape, 1)
    at_target = jnp.sum(jnp.where(place_ref[...] == places, logits, 0.0), axis=1, keepdims=True)
    exps_ref[...] = shifted.astype(bf16)
    same = eye()
    lanes = [jnp.sum(jnp.where(same, v, 0.0), axis=0, keepdims=True) for v in (lse, top, at_target)]
    facts = jnp.concatenate(lanes + [rows_ref[...], jnp.zeros((3, TOK), f32)], axis=0)
    for k in range(32):
        facts_ref[k] = facts


def combine_kernel(facts_ref, o_ref):
    rows = []
    for b in range(BINS):
        part = jnp.concatenate([facts_ref[8 * b + k][0:1] for k in range(8)], axis=0)
        top = jnp.max(part, axis=0, keepdims=True)
        rows.append(top + jnp.log(jnp.sum(jnp.exp(part - top), axis=0, keepdims=True)))
    rows = jnp.concatenate(rows, axis=0)
    for k in range(16):
        o_ref[k] = rows


def grad_kernel(where_ref, lse_ref, facts_ref, exps0, exps1, exps2, exps3, head_ref, grads_ref, kept_ref, sent_ref, norms_ref):
    lse = lse_ref[...]
    top = jnp.max(lse, axis=0)
    log_norm = top + jnp.log(jnp.sum(jnp.exp(lse - top[None]), axis=0))
    same = eye()

    def column(row):
        return jnp.sum(jnp.where(same, row, 0.0), axis=1, keepdims=True)

    norms_ref[...] = log_norm
    places = lax.broadcasted_iota(i32, exps0.shape, 1) + where_ref[1]
    for r, exps_ref in enumerate([exps0, exps1, exps2, exps3]):
        b = lax.rem(where_ref[2] + r, BINS)
        mine = facts_ref[8 * b + where_ref[0]]
        norm = norms_ref[pl.ds(b, 1)]
        scale = column(mine[3:4] * jnp.exp(mine[1:2] - norm))
        hit = column(mine[3:4] * (jnp.exp(mine[2:3] - norm) - 1.0))
        target = column(mine[4:5]).astype(i32)
        grads = jnp.where(target == places, hit, exps_ref[...].astype(f32) * scale).astype(bf16)
        grads_ref[b] = grads
        half = head_ref.shape[0] // 2
        for h, ref in ((1, sent_ref), (0, kept_ref)):
            terms = lax.dot_general(
                head_ref[h * half : (h + 1) * half],
                grads,
                (((1,), (1,)), ((), ())),
                preferred_element_type=f32,
            )
            for p in range(16):
                ref[b, p] = packed(terms[COLS * p : COLS * (p + 1)]).astype(ref.dtype)


def column_order(width):
    half = width // 2
    p = lax.broadcasted_iota(i32, (width, 1), 0)
    core = lax.rem(lax.axis_index("c") + p // half, 2)
    q = lax.rem(p, half)
    natural = lax.rem(q // COLS, 4) * (8 * COLS) + q // (4 * COLS) * (2 * COLS) + core * COLS + lax.rem(q, COLS)
    return (natural == lax.broadcasted_iota(i32, (1, width), 1)).astype(bf16)


def dot(a, b, ca, cb):
    return lax.dot_general(a, b, (((ca,), (cb,)), ((), ())), preferred_element_type=f32)


def body(hidden, head, targets, segments, loss_mask):
    vocab_rows, width = head.shape
    half, hw = TOK // 2, width // 2
    y = lax.axis_index("y")
    at = [lax.rem(y + r, BINS) for r in range(BINS)]

    spread = call(pack_kernel, shape(16, 64, 128, dtype=bf16), [VMEM], hidden.T)
    along_z = exchange(spread, Z).reshape(BINS, 1, 4, 64, 128)
    own_packed = exchange(
        jnp.broadcast_to(along_z, (BINS, 4, 4, 64, 128)).reshape(16, 4, 64, 128), ("y", "x")
    ).reshape(BINS, 16, 64, 128)
    other_packed = swap_core(own_packed)
    order = column_order(width)
    head_t = dot(order, head, 1, 1).astype(bf16)
    unpack = functools.partial(
        call, unpack_kernel, shape(BINS, hw, TOK, dtype=bf16), [VMEM], nbytes=4 * 2**20
    )
    own_cols = unpack(own_packed)
    own_cols, head_t, other_packed = lax.optimization_barrier((own_cols, head_t, other_packed))
    other_cols = unpack(other_packed)

    def pick(a, b):
        return lax.dynamic_index_in_dim(a, b, 0, keepdims=False)

    def partial_logits(r):
        return dot(pick(own_cols, at[r]), head_t[:hw], 0, 0) + dot(pick(other_cols, at[r]), head_t[hw:], 0, 0)

    far = partial_logits(2)
    from_left = shift(far[:half], 1)
    from_right = shift(far[half:], 3)
    up = partial_logits(1)
    down = partial_logits(3)
    own = partial_logits(0)
    nothing = jnp.zeros((half, vocab_rows), f32)
    up = shift(up + jnp.concatenate([from_left, nothing]), 1)
    down = shift(down + jnp.concatenate([nothing, from_right]), 3)

    mask_f = loss_mask[0].astype(f32)
    seg_ids = segments[0]
    same = (seg_ids[:, None] == seg_ids[None, :]).astype(f32)
    counts = jnp.sum(same * mask_f[None, :], axis=1)
    weight = loss_scale * mask_f / jnp.maximum(counts, 1.0)
    shard = ((lax.axis_index("zh") * 4 + lax.axis_index("zl")) * 4 + lax.axis_index("x")) * 2
    vocab_start = (shard + lax.axis_index("c")) * vocab_rows
    place = (targets[0] - vocab_start)[:, None]
    rows = jnp.stack([weight, targets[0].astype(f32)])
    here = jnp.stack([lax.axis_index("x") * 2 + lax.axis_index("c"), vocab_start, y]).astype(i32)

    exps, facts = call(
        softmax_kernel,
        [shape(TOK, vocab_rows, dtype=bf16), shape(32, 8, TOK)],
        [VMEM] * 3,
        own + up + down,
        place,
        rows,
    )
    exps, facts, own_cols, other_cols = lax.optimization_barrier((exps, facts, own_cols, other_cols))

    every_exp = [exps, shift(exps, 3), shift(exps, 2), shift(exps, 1)]
    facts = exchange(facts, ("y", "x", "c"))
    lse = exchange(call(combine_kernel, shape(16, BINS, TOK), [VMEM], facts), Z)
    lse, facts, every_exp = lax.optimization_barrier((lse, facts, every_exp))

    features = jnp.concatenate(
        [
            (dot(own_cols[b], order[:hw], 0, 0) + dot(other_cols[b], order[hw:], 0, 0)).astype(bf16)
            for b in range(BINS)
        ]
    )

    grads, kept, sent = call(
        grad_kernel,
        [
            shape(BINS, TOK, vocab_rows, dtype=bf16),
            shape(BINS, 16, 64, 128),
            shape(BINS, 16, 64, 128, dtype=bf16),
        ],
        [SMEM] + [VMEM] * 7,
        here,
        lse,
        facts,
        *every_exp,
        head_t,
        scratch=[pltpu.VMEM((BINS, TOK), f32)],
    )
    terms = swap_core(sent)
    grad_head = dot(grads.reshape(BINS * TOK, vocab_rows), features, 0, 0).astype(bf16)
    terms, grad_head = lax.optimization_barrier((terms, grad_head))
    terms = (kept + terms.astype(f32)).astype(bf16).reshape(16, 4, 64, 128)
    terms = exchange(terms, ("y", "x")).reshape(BINS, 4, 4, 64, 128)
    terms = jnp.sum(terms.astype(f32), axis=1).astype(bf16).reshape(16, 64, 128)
    terms = exchange(terms, Z)
    grad_hidden = unpacked(jnp.sum(terms.astype(f32), axis=0)).astype(bf16).T
    return (grad_hidden, grad_head)


def solution(mesh):
    fine = Mesh(mesh.devices.reshape(4, 4, 4, 4, 2), EVERY)
    placed = (P("y", ROW), P(ROW, "y"), P("y", None), P("y", None), P("y", None))
    return jax.shard_map(
        body,
        mesh=fine,
        in_specs=placed,
        out_specs=(P("y", ROW), P(ROW, "y")),
        check_vma=False,
    )
```

```python
import functools

import jax
import jax.numpy as jnp
from jax import lax
from jax.experimental import pallas as pl
from jax.experimental.pallas import tpu as pltpu
from jax.sharding import Mesh
from jax.sharding import PartitionSpec as P

loss_scale = 256.0
BINS = 4
EVERY = ("y", "zh", "zl", "x", "c")
ROW = ("zh", "zl", "x", "c")
Z = ("zh", "zl")
COLS, TOK, HIGH, EXTRA = 40, 192, 64, 24
f32, bf16, i32 = jnp.float32, jnp.bfloat16, jnp.int32
VMEM = pl.BlockSpec(memory_space=pltpu.VMEM)
FREE = pl.BlockSpec()
SMEM = pl.BlockSpec(memory_space=pltpu.SMEM)


def shift(a, k):
    return lax.ppermute(a, "y", [(i, (i + k) % BINS) for i in range(BINS)])


def swap_core(a):
    return lax.ppermute(a, "c", [(0, 1), (1, 0)])


def exchange(a, axes):
    return lax.all_to_all(a, axes, 0, 0, tiled=True)


def call(kernel, out, ins, *args, flops=0, nbytes=0, scratch=()):
    return pl.pallas_call(
        kernel,
        out_shape=out,
        in_specs=ins,
        scratch_shapes=list(scratch),
        out_specs=[VMEM] * len(out) if isinstance(out, (list, tuple)) else VMEM,
        compiler_params=pltpu.CompilerParams(vmem_limit_bytes=16 * 2**20),
        cost_estimate=pl.CostEstimate(flops=flops, bytes_accessed=nbytes, transcendentals=0),
    )(*args)


def shape(*dims, dtype=f32):
    return jax.ShapeDtypeStruct(dims, dtype)


def packed(piece):
    tail = piece[:, 128:]
    right = jnp.concatenate([tail[EXTRA:], jnp.zeros((2 * EXTRA - COLS, TOK - 128), f32)], axis=0)
    return jnp.concatenate([piece[:, :128], jnp.concatenate([tail[:EXTRA], right], axis=1)], axis=0)


def unpacked(piece):
    tail = jnp.concatenate([piece[COLS:, :64], piece[COLS : 2 * COLS - EXTRA, 64:]], axis=0)
    return jnp.concatenate([piece[:COLS], tail], axis=1)


def pack_kernel(h_ref, o_ref):
    piece = packed(h_ref[...].astype(f32)).astype(bf16)
    for k in range(16):
        o_ref[k] = piece


def unpack_kernel(a_ref, o_ref):
    def one(b, _):
        for p in range(8):
            pair = [unpacked(a_ref[b, 2 * p + k].astype(f32)) for k in range(2)]
            o_ref[b, 2 * COLS * p : 2 * COLS * (p + 1), :] = jnp.concatenate(pair, axis=0).astype(bf16)
        return 0

    lax.fori_loop(0, BINS, one, 0)


def eye():
    return lax.broadcasted_iota(i32, (TOK, TOK), 0) == lax.broadcasted_iota(i32, (TOK, TOK), 1)


def softmax_kernel(logits_ref, place_ref, rows_ref, exps_ref, facts_ref):
    logits = logits_ref[...]
    top = jnp.max(logits, axis=1, keepdims=True)
    shifted = jnp.exp(logits - top)
    total = jnp.sum(shifted, axis=1, keepdims=True)
    lse = top + jnp.log(total)
    places = lax.broadcasted_iota(i32, logits.shape, 1)
    at_target = jnp.sum(jnp.where(place_ref[...] == places, logits, 0.0), axis=1, keepdims=True)
    exps_ref[...] = (shifted * (1.0 / total)).astype(bf16)
    same = eye()
    lanes = [jnp.sum(jnp.where(same, v, 0.0), axis=0, keepdims=True) for v in (lse, at_target)]
    facts = jnp.concatenate(lanes + [rows_ref[...]], axis=0)
    for k in range(32):
        facts_ref[k] = facts


def combine_kernel(facts_ref, o_ref):
    rows = []
    for b in range(BINS):
        part = jnp.concatenate([facts_ref[8 * b + k][0:1] for k in range(8)], axis=0)
        top = jnp.max(part, axis=0, keepdims=True)
        rows.append(top + jnp.log(jnp.sum(jnp.exp(part - top), axis=0, keepdims=True)))
    rows = jnp.concatenate(rows, axis=0)
    for k in range(16):
        o_ref[k] = rows


def grad_kernel(where_ref, lse_ref, facts_ref, exps0, exps1, exps2, exps3, head_ref, grads_ref, kept_ref, sent_ref, norms_ref):
    lse = lse_ref[...]
    top = jnp.max(lse, axis=0)
    log_norm = top + jnp.log(jnp.sum(jnp.exp(lse - top[None]), axis=0))
    same = eye()

    def column(row):
        return jnp.sum(jnp.where(same, row, 0.0), axis=1, keepdims=True)

    norms_ref[...] = log_norm
    places = lax.broadcasted_iota(i32, exps0.shape, 1) + where_ref[1]
    for r, exps_ref in enumerate([exps0, exps1, exps2, exps3]):
        b = lax.rem(where_ref[2] + r, BINS)
        mine = facts_ref[8 * b + where_ref[0]]
        norm = norms_ref[pl.ds(b, 1)]
        scale = column(mine[2:3] * jnp.exp(mine[0:1] - norm))
        hit = column(mine[2:3] * (jnp.exp(mine[1:2] - norm) - 1.0))
        target = column(mine[3:4]).astype(i32)
        grads = jnp.where(target == places, hit, exps_ref[...].astype(f32) * scale).astype(bf16)
        grads_ref[b] = grads
        half = head_ref.shape[0] // 2
        for h, ref in ((1, sent_ref), (0, kept_ref)):
            terms = lax.dot_general(
                head_ref[h * half : (h + 1) * half],
                grads,
                (((1,), (1,)), ((), ())),
                preferred_element_type=f32,
            )
            for p in range(16):
                ref[b, p] = packed(terms[COLS * p : COLS * (p + 1)]).astype(ref.dtype)


def head_kernel(own_ref, other_ref, grads_ref, o_ref):
    half = own_ref.shape[1]
    for h, ref in enumerate([own_ref, other_ref]):
        total = sum(jnp.dot(ref[b], grads_ref[b], preferred_element_type=f32) for b in range(BINS))
        o_ref[h * half : (h + 1) * half, :] = total.astype(bf16)


def column_order(width):
    half = width // 2
    p = lax.broadcasted_iota(i32, (width, 1), 0)
    core = lax.rem(lax.axis_index("c") + p // half, 2)
    q = lax.rem(p, half)
    natural = lax.rem(q // COLS, 4) * (8 * COLS) + q // (4 * COLS) * (2 * COLS) + core * COLS + lax.rem(q, COLS)
    return (natural == lax.broadcasted_iota(i32, (1, width), 1)).astype(bf16)


def dot(a, b, ca, cb):
    return lax.dot_general(a, b, (((ca,), (cb,)), ((), ())), preferred_element_type=f32)


def body(hidden, head, targets, segments, loss_mask):
    vocab_rows, width = head.shape
    half, hw = TOK // 2, width // 2
    y = lax.axis_index("y")
    at = [lax.rem(y + r, BINS) for r in range(BINS)]

    spread = call(pack_kernel, shape(16, 64, 128, dtype=bf16), [VMEM], hidden.T)
    along_z = exchange(spread, Z).reshape(BINS, 1, 4, 64, 128)
    own_packed = exchange(
        jnp.broadcast_to(along_z, (BINS, 4, 4, 64, 128)).reshape(16, 4, 64, 128), ("y", "x")
    ).reshape(BINS, 16, 64, 128)
    order = column_order(width)
    head_t = dot(order, head, 1, 1).astype(bf16)
    own_packed, head_t = lax.optimization_barrier((own_packed, head_t))
    other_packed = swap_core(own_packed)
    unpack = functools.partial(
        call, unpack_kernel, shape(BINS, hw, TOK, dtype=bf16), [VMEM], nbytes=4 * 2**20
    )
    own_cols = unpack(own_packed)
    own_cols, other_packed = lax.optimization_barrier((own_cols, other_packed))
    other_cols = unpack(other_packed)

    def pick(a, b):
        return lax.dynamic_index_in_dim(a, b, 0, keepdims=False)

    def partial_logits(r):
        return dot(pick(own_cols, at[r]), head_t[:hw], 0, 0) + dot(pick(other_cols, at[r]), head_t[hw:], 0, 0)

    far = partial_logits(2)
    from_left = shift(far[:half], 1)
    from_right = shift(far[half:], 3)
    up = partial_logits(1)
    down = partial_logits(3)
    own = partial_logits(0)
    nothing = jnp.zeros((half, vocab_rows), f32)
    up = shift(up + jnp.concatenate([from_left, nothing]), 1)
    down = shift(down + jnp.concatenate([nothing, from_right]), 3)

    mask_f = loss_mask[0].astype(f32)
    seg_ids = segments[0]
    same = (seg_ids[:, None] == seg_ids[None, :]).astype(f32)
    counts = jnp.sum(same * mask_f[None, :], axis=1)
    weight = loss_scale * mask_f / jnp.maximum(counts, 1.0)
    shard = ((lax.axis_index("zh") * 4 + lax.axis_index("zl")) * 4 + lax.axis_index("x")) * 2
    vocab_start = (shard + lax.axis_index("c")) * vocab_rows
    place = (targets[0] - vocab_start)[:, None]
    rows = jnp.stack([weight, targets[0].astype(f32)])
    here = jnp.stack([lax.axis_index("x") * 2 + lax.axis_index("c"), vocab_start, y]).astype(i32)

    exps, facts = call(
        softmax_kernel,
        [shape(TOK, vocab_rows, dtype=bf16), shape(32, 4, TOK)],
        [VMEM] * 3,
        own + up + down,
        place,
        rows,
    )
    exps, facts = lax.optimization_barrier((exps, facts))

    every_exp = [exps, shift(exps, 3), shift(exps, 2), shift(exps, 1)]
    facts = exchange(facts, ("y", "x", "c"))
    lse = exchange(call(combine_kernel, shape(16, BINS, TOK), [VMEM], facts), Z)
    lse, facts, every_exp = lax.optimization_barrier((lse, facts, every_exp))

    grads, kept, sent = call(
        grad_kernel,
        [
            shape(BINS, TOK, vocab_rows, dtype=bf16),
            shape(BINS, 16, 64, 128),
            shape(BINS, 16, 64, 128, dtype=bf16),
        ],
        [SMEM] + [VMEM] * 6 + [FREE],
        here,
        lse,
        facts,
        *every_exp,
        head_t,
        scratch=[pltpu.VMEM((BINS, TOK), f32)],
    )
    terms = swap_core(sent)
    head_terms = call(
        head_kernel, shape(width, vocab_rows, dtype=bf16), [FREE, FREE, VMEM], own_cols, other_cols, grads, flops=2 * 10**9
    )
    terms, head_terms = lax.optimization_barrier((terms, head_terms))
    terms = (kept + terms.astype(f32)).astype(bf16).reshape(16, 4, 64, 128)
    terms = exchange(terms, ("y", "x")).reshape(BINS, 4, 4, 64, 128)
    terms = jnp.sum(terms.astype(f32), axis=1).astype(bf16).reshape(16, 64, 128)
    terms = exchange(terms, Z)
    grad_hidden = unpacked(jnp.sum(terms.astype(f32), axis=0)).astype(bf16).T
    grad_head = dot(head_terms, order, 0, 0).astype(bf16)
    return (grad_hidden, grad_head)


def solution(mesh):
    fine = Mesh(mesh.devices.reshape(4, 4, 4, 4, 2), EVERY)
    placed = (P("y", ROW), P(ROW, "y"), P("y", None), P("y", None), P("y", None))
    return jax.shard_map(
        body,
        mesh=fine,
        in_specs=placed,
        out_specs=(P("y", ROW), P(ROW, "y")),
        check_vma=False,
    )
```

```python
import functools

import jax
import jax.numpy as jnp
from jax import lax
from jax.experimental import pallas as pl
from jax.experimental.pallas import tpu as pltpu
from jax.sharding import Mesh
from jax.sharding import PartitionSpec as P

loss_scale = 256.0
BINS = 4
EVERY = ("y", "zh", "zl", "x", "c")
ROW = ("zh", "zl", "x", "c")
Z = ("zh", "zl")
COLS, TOK, HIGH, EXTRA = 40, 192, 64, 24
f32, bf16, i32 = jnp.float32, jnp.bfloat16, jnp.int32
VMEM = pl.BlockSpec(memory_space=pltpu.VMEM)
FREE = pl.BlockSpec()
SMEM = pl.BlockSpec(memory_space=pltpu.SMEM)


def shift(a, k):
    return lax.ppermute(a, "y", [(i, (i + k) % BINS) for i in range(BINS)])


def swap_core(a):
    return lax.ppermute(a, "c", [(0, 1), (1, 0)])


def exchange(a, axes):
    return lax.all_to_all(a, axes, 0, 0, tiled=True)


def call(kernel, out, ins, *args, flops=0, nbytes=0, scratch=()):
    return pl.pallas_call(
        kernel,
        out_shape=out,
        in_specs=ins,
        scratch_shapes=list(scratch),
        out_specs=[VMEM] * len(out) if isinstance(out, (list, tuple)) else VMEM,
        compiler_params=pltpu.CompilerParams(vmem_limit_bytes=16 * 2**20),
        cost_estimate=pl.CostEstimate(flops=flops, bytes_accessed=nbytes, transcendentals=0),
    )(*args)


def shape(*dims, dtype=f32):
    return jax.ShapeDtypeStruct(dims, dtype)


def packed(piece):
    tail = piece[:, 128:]
    right = jnp.concatenate([tail[EXTRA:], jnp.zeros((2 * EXTRA - COLS, TOK - 128), f32)], axis=0)
    return jnp.concatenate([piece[:, :128], jnp.concatenate([tail[:EXTRA], right], axis=1)], axis=0)


def unpacked(piece):
    tail = jnp.concatenate([piece[COLS:, :64], piece[COLS : 2 * COLS - EXTRA, 64:]], axis=0)
    return jnp.concatenate([piece[:COLS], tail], axis=1)


def pack_kernel(h_ref, o_ref):
    piece = packed(h_ref[...].astype(f32)).astype(bf16)
    for k in range(16):
        o_ref[k] = piece


def unpack_kernel(a_ref, o_ref):
    def one(b, _):
        for p in range(8):
            pair = [unpacked(a_ref[b, 2 * p + k].astype(f32)) for k in range(2)]
            o_ref[b, 2 * COLS * p : 2 * COLS * (p + 1), :] = jnp.concatenate(pair, axis=0).astype(bf16)
        return 0

    lax.fori_loop(0, BINS, one, 0)


def eye():
    return lax.broadcasted_iota(i32, (TOK, TOK), 0) == lax.broadcasted_iota(i32, (TOK, TOK), 1)


def softmax_kernel(logits_ref, place_ref, row_ref, exps_ref, lse_ref, facts_ref):
    logits = logits_ref[...]
    top = jnp.max(logits, axis=1, keepdims=True)
    shifted = jnp.exp(logits - top)
    total = jnp.sum(shifted, axis=1, keepdims=True)
    lse = top + jnp.log(total)
    places = lax.broadcasted_iota(i32, logits.shape, 1)
    at_target = jnp.sum(jnp.where(place_ref[...] == places, logits, 0.0), axis=1, keepdims=True)
    exps_ref[...] = (shifted * (1.0 / total)).astype(bf16)
    same = eye()
    lanes = [jnp.sum(jnp.where(same, v, 0.0), axis=0, keepdims=True) for v in (lse, at_target)]
    facts_ref[...] = jnp.concatenate(lanes + [row_ref[...]], axis=0)
    for k in range(16):
        lse_ref[k] = lanes[0]


def log_sum_exp(part):
    top = jnp.max(part, axis=0, keepdims=True)
    return top + jnp.log(jnp.sum(jnp.exp(part - top), axis=0, keepdims=True))


def combine_kernel(lse_ref, facts_ref, o_ref):
    total = log_sum_exp(jnp.concatenate([lse_ref[k] for k in range(16)], axis=0))
    rows = jnp.concatenate([total, facts_ref[...]], axis=0)
    for k in range(32):
        o_ref[k] = rows


def put_terms(columns, grads, ref, b):
    terms = lax.dot_general(columns, grads, (((1,), (1,)), ((), ())), preferred_element_type=f32)
    for p in range(16):
        ref[b, p] = packed(terms[COLS * p : COLS * (p + 1)]).astype(ref.dtype)


def grad_kernel(where_ref, facts_ref, exps0, exps1, exps2, exps3, head_ref, grads_ref, sent_ref):
    same = eye()

    def column(row):
        return jnp.sum(jnp.where(same, row, 0.0), axis=1, keepdims=True)

    half = head_ref.shape[0] // 2
    places = lax.broadcasted_iota(i32, exps0.shape, 1) + where_ref[1]
    for r, exps_ref in enumerate([exps0, exps1, exps2, exps3]):
        b = lax.rem(where_ref[2] + r, BINS)
        norm = log_sum_exp(jnp.concatenate([facts_ref[8 * b + k][0:1] for k in range(8)], axis=0))
        mine = facts_ref[8 * b + where_ref[0]]
        code = mine[3:4].astype(i32)
        counts = (code & 63).astype(f32)
        weight = jnp.where(counts > 0, loss_scale / jnp.maximum(counts, 1.0), 0.0)
        scale = column(weight * jnp.exp(mine[1:2] - norm))
        hit = column(weight * (jnp.exp(mine[2:3] - norm) - 1.0))
        target = column((code >> 6).astype(f32)).astype(i32)
        grads = jnp.where(target == places, hit, exps_ref[...].astype(f32) * scale).astype(bf16)
        grads_ref[b] = grads
        put_terms(head_ref[half:], grads, sent_ref, b)


def kept_kernel(head_ref, grads_ref, kept_ref):
    for b in range(BINS):
        put_terms(head_ref[: head_ref.shape[0] // 2], grads_ref[b], kept_ref, b)


def head_kernel(own_ref, other_ref, grads_ref, o_ref):
    half = own_ref.shape[1]
    for h, ref in enumerate([own_ref, other_ref]):
        total = sum(jnp.dot(ref[b], grads_ref[b], preferred_element_type=f32) for b in range(BINS))
        o_ref[h * half : (h + 1) * half, :] = total.astype(bf16)


def column_order(width):
    half = width // 2
    p = lax.broadcasted_iota(i32, (width, 1), 0)
    core = lax.rem(lax.axis_index("c") + p // half, 2)
    q = lax.rem(p, half)
    natural = lax.rem(q // COLS, 4) * (8 * COLS) + q // (4 * COLS) * (2 * COLS) + core * COLS + lax.rem(q, COLS)
    return (natural == lax.broadcasted_iota(i32, (1, width), 1)).astype(bf16)


def dot(a, b, ca, cb):
    return lax.dot_general(a, b, (((ca,), (cb,)), ((), ())), preferred_element_type=f32)


def body(hidden, head, targets, segments, loss_mask):
    vocab_rows, width = head.shape
    half, hw = TOK // 2, width // 2
    y = lax.axis_index("y")
    at = [lax.rem(y + r, BINS) for r in range(BINS)]

    spread = call(pack_kernel, shape(16, 64, 128, dtype=bf16), [VMEM], hidden.T)
    along_z = exchange(spread, Z).reshape(BINS, 1, 4, 64, 128)
    own_packed = exchange(
        jnp.broadcast_to(along_z, (BINS, 4, 4, 64, 128)).reshape(16, 4, 64, 128), ("y", "x")
    ).reshape(BINS, 16, 64, 128)
    order = column_order(width)
    head_t = dot(order, head, 1, 1).astype(bf16)
    own_packed, head_t = lax.optimization_barrier((own_packed, head_t))
    other_packed = swap_core(own_packed)
    unpack = functools.partial(
        call, unpack_kernel, shape(BINS, hw, TOK, dtype=bf16), [VMEM], nbytes=4 * 2**20
    )
    own_cols = unpack(own_packed)
    own_cols, other_packed = lax.optimization_barrier((own_cols, other_packed))
    other_cols = unpack(other_packed)

    def pick(a, b):
        return lax.dynamic_index_in_dim(a, b, 0, keepdims=False)

    def partial_logits(r):
        return dot(pick(own_cols, at[r]), head_t[:hw], 0, 0) + dot(pick(other_cols, at[r]), head_t[hw:], 0, 0)

    far = partial_logits(2)
    from_left = shift(far[:half], 1)
    from_right = shift(far[half:], 3)
    up = partial_logits(1)
    down = partial_logits(3)
    own = partial_logits(0)
    up, down = lax.optimization_barrier((up, down))
    nothing = jnp.zeros((half, vocab_rows), f32)
    up = shift(up + jnp.concatenate([from_left, nothing]), 1)
    down = shift(down + jnp.concatenate([nothing, from_right]), 3)

    mask_f = loss_mask[0].astype(f32)
    seg_ids = segments[0]
    same = (seg_ids[:, None] == seg_ids[None, :]).astype(f32)
    counts = jnp.sum(same * mask_f[None, :], axis=1)
    shard = ((lax.axis_index("zh") * 4 + lax.axis_index("zl")) * 4 + lax.axis_index("x")) * 2
    vocab_start = (shard + lax.axis_index("c")) * vocab_rows
    place = (targets[0] - vocab_start)[:, None]
    row = (64 * targets + loss_mask * counts.astype(i32)[None]).astype(f32)
    here = jnp.stack([lax.axis_index("x") * 2 + lax.axis_index("c"), vocab_start, y]).astype(i32)

    exps, lse, facts = call(
        softmax_kernel,
        [shape(TOK, vocab_rows, dtype=bf16), shape(16, 1, TOK), shape(3, TOK)],
        [VMEM] * 3,
        own + up + down,
        place,
        row,
    )
    exps, lse = lax.optimization_barrier((exps, lse))

    every_exp = [exps, shift(exps, 3), shift(exps, 2), shift(exps, 1)]
    facts = call(combine_kernel, shape(32, 4, TOK), [VMEM] * 2, exchange(lse, Z), facts)
    facts = exchange(facts, ("y", "x", "c"))
    facts, every_exp = lax.optimization_barrier((facts, every_exp))

    grads, sent = call(
        grad_kernel,
        [shape(BINS, TOK, vocab_rows, dtype=bf16), shape(BINS, 16, 64, 128, dtype=bf16)],
        [SMEM] + [VMEM] * 5 + [FREE],
        here,
        facts,
        *every_exp,
        head_t,
    )
    terms = swap_core(sent)
    kept = call(kept_kernel, shape(BINS, 16, 64, 128), [FREE, VMEM], head_t, grads, flops=10**9)
    head_terms = call(
        head_kernel, shape(width, vocab_rows, dtype=bf16), [FREE, FREE, VMEM], own_cols, other_cols, grads, flops=2 * 10**9
    )
    terms, kept = lax.optimization_barrier((terms, kept))
    terms = (kept + terms.astype(f32)).astype(bf16).reshape(16, 4, 64, 128)
    terms = exchange(terms, ("y", "x")).reshape(BINS, 4, 4, 64, 128)
    terms = jnp.sum(terms.astype(f32), axis=1).astype(bf16).reshape(16, 64, 128)
    terms = exchange(terms, Z)
    grad_hidden = unpacked(jnp.sum(terms.astype(f32), axis=0)).astype(bf16).T
    grad_head = dot(head_terms, order, 0, 0).astype(bf16)
    return (grad_hidden, grad_head)


def solution(mesh):
    fine = Mesh(mesh.devices.reshape(4, 4, 4, 4, 2), EVERY)
    placed = (P("y", ROW), P(ROW, "y"), P("y", None), P("y", None), P("y", None))
    return jax.shard_map(
        body,
        mesh=fine,
        in_specs=placed,
        out_specs=(P("y", ROW), P(ROW, "y")),
        check_vma=False,
    )
```

```python
import functools

import jax
import jax.numpy as jnp
from jax import lax
from jax.experimental import pallas as pl
from jax.experimental.pallas import tpu as pltpu
from jax.sharding import Mesh
from jax.sharding import PartitionSpec as P

loss_scale = 256.0
BINS = 4
EVERY = ("y", "zh", "zl", "x", "c")
ROW = ("zh", "zl", "x", "c")
Z = ("zh", "zl")
COLS, TOK, HIGH, EXTRA = 40, 192, 64, 24
f32, bf16, i32 = jnp.float32, jnp.bfloat16, jnp.int32
VMEM = pl.BlockSpec(memory_space=pltpu.VMEM)
FREE = pl.BlockSpec()
SMEM = pl.BlockSpec(memory_space=pltpu.SMEM)


def shift(a, k):
    return lax.ppermute(a, "y", [(i, (i + k) % BINS) for i in range(BINS)])


def swap_core(a):
    return lax.ppermute(a, "c", [(0, 1), (1, 0)])


def exchange(a, axes):
    return lax.all_to_all(a, axes, 0, 0, tiled=True)


def call(kernel, out, ins, *args, flops=0, nbytes=0, scratch=()):
    return pl.pallas_call(
        kernel,
        out_shape=out,
        in_specs=ins,
        scratch_shapes=list(scratch),
        out_specs=[VMEM] * len(out) if isinstance(out, (list, tuple)) else VMEM,
        compiler_params=pltpu.CompilerParams(vmem_limit_bytes=16 * 2**20),
        cost_estimate=pl.CostEstimate(flops=flops, bytes_accessed=nbytes, transcendentals=0),
    )(*args)


def shape(*dims, dtype=f32):
    return jax.ShapeDtypeStruct(dims, dtype)


def packed(piece):
    tail = piece[:, 128:]
    right = jnp.concatenate([tail[EXTRA:], jnp.zeros((2 * EXTRA - COLS, TOK - 128), f32)], axis=0)
    return jnp.concatenate([piece[:, :128], jnp.concatenate([tail[:EXTRA], right], axis=1)], axis=0)


def unpacked(piece):
    tail = jnp.concatenate([piece[COLS:, :64], piece[COLS : 2 * COLS - EXTRA, 64:]], axis=0)
    return jnp.concatenate([piece[:COLS], tail], axis=1)


def pack_kernel(h_ref, o_ref):
    piece = packed(h_ref[...].astype(f32)).astype(bf16)
    for k in range(16):
        o_ref[k] = piece


def unpack_kernel(a_ref, o_ref):
    def one(b, _):
        for p in range(8):
            pair = [unpacked(a_ref[b, 2 * p + k].astype(f32)) for k in range(2)]
            o_ref[b, 2 * COLS * p : 2 * COLS * (p + 1), :] = jnp.concatenate(pair, axis=0).astype(bf16)
        return 0

    lax.fori_loop(0, BINS, one, 0)


def eye():
    return lax.broadcasted_iota(i32, (TOK, TOK), 0) == lax.broadcasted_iota(i32, (TOK, TOK), 1)


def softmax_kernel(logits_ref, place_ref, row_ref, exps_ref, lse_ref, facts_ref):
    logits = logits_ref[...]
    top = jnp.max(logits, axis=1, keepdims=True)
    shifted = jnp.exp(logits - top)
    total = jnp.sum(shifted, axis=1, keepdims=True)
    lse = top + jnp.log(total)
    places = lax.broadcasted_iota(i32, logits.shape, 1)
    at_target = jnp.sum(jnp.where(place_ref[...] == places, logits, 0.0), axis=1, keepdims=True)
    exps_ref[...] = (shifted * (1.0 / total)).astype(bf16)
    same = eye()
    lanes = [jnp.sum(jnp.where(same, v, 0.0), axis=0, keepdims=True) for v in (lse, at_target)]
    facts_ref[...] = jnp.concatenate(lanes + [row_ref[...]], axis=0)
    for k in range(16):
        lse_ref[k] = lanes[0]


def log_sum_exp(part):
    top = jnp.max(part, axis=0, keepdims=True)
    return top + jnp.log(jnp.sum(jnp.exp(part - top), axis=0, keepdims=True))


def combine_kernel(lse_ref, facts_ref, o_ref):
    total = log_sum_exp(jnp.concatenate([lse_ref[k] for k in range(16)], axis=0))
    rows = jnp.concatenate([total, facts_ref[...]], axis=0)
    for k in range(32):
        o_ref[k] = rows


def put_terms(columns, grads, ref, b):
    terms = lax.dot_general(columns, grads, (((1,), (1,)), ((), ())), preferred_element_type=f32)
    for p in range(16):
        ref[b, p] = packed(terms[COLS * p : COLS * (p + 1)]).astype(ref.dtype)


def grad_kernel(where_ref, facts_ref, exps0, exps1, exps2, exps3, head_ref, grads_ref, sent_ref):
    same = eye()

    def column(row):
        return jnp.sum(jnp.where(same, row, 0.0), axis=1, keepdims=True)

    half = head_ref.shape[0] // 2
    places = lax.broadcasted_iota(i32, exps0.shape, 1) + where_ref[1]
    for r, exps_ref in enumerate([exps0, exps1, exps2, exps3]):
        b = lax.rem(where_ref[2] + r, BINS)
        norm = log_sum_exp(jnp.concatenate([facts_ref[8 * b + k][0:1] for k in range(8)], axis=0))
        mine = facts_ref[8 * b + where_ref[0]]
        code = mine[3:4].astype(i32)
        counts = (code & 63).astype(f32)
        weight = jnp.where(counts > 0, loss_scale / jnp.maximum(counts, 1.0), 0.0)
        scale = column(weight * jnp.exp(mine[1:2] - norm))
        hit = column(weight * (jnp.exp(mine[2:3] - norm) - 1.0))
        target = column((code >> 6).astype(f32)).astype(i32)
        grads = jnp.where(target == places, hit, exps_ref[...].astype(f32) * scale).astype(bf16)
        grads_ref[b] = grads
        put_terms(head_ref[half:], grads, sent_ref, b)


def kept_kernel(head_ref, grads_ref, kept_ref):
    for b in range(BINS):
        put_terms(head_ref[: head_ref.shape[0] // 2], grads_ref[b], kept_ref, b)


def head_kernel(own_ref, other_ref, grads_ref, o_ref):
    half = own_ref.shape[1]
    for h, ref in enumerate([own_ref, other_ref]):
        total = sum(jnp.dot(ref[b], grads_ref[b], preferred_element_type=f32) for b in range(BINS))
        o_ref[h * half : (h + 1) * half, :] = total.astype(bf16)


def column_order(width):
    half = width // 2
    p = lax.broadcasted_iota(i32, (width, 1), 0)
    core = lax.rem(lax.axis_index("c") + p // half, 2)
    q = lax.rem(p, half)
    natural = lax.rem(q // COLS, 4) * (8 * COLS) + q // (4 * COLS) * (2 * COLS) + core * COLS + lax.rem(q, COLS)
    return (natural == lax.broadcasted_iota(i32, (1, width), 1)).astype(bf16)


def dot(a, b, ca, cb):
    return lax.dot_general(a, b, (((ca,), (cb,)), ((), ())), preferred_element_type=f32)


def body(hidden, head, targets, segments, loss_mask):
    vocab_rows, width = head.shape
    half, hw = TOK // 2, width // 2
    y = lax.axis_index("y")
    at = [lax.rem(y + r, BINS) for r in range(BINS)]

    spread = call(pack_kernel, shape(16, 64, 128, dtype=bf16), [VMEM], hidden.T)
    along_z = exchange(spread, Z).reshape(BINS, 1, 4, 64, 128)
    own_packed = exchange(
        jnp.broadcast_to(along_z, (BINS, 4, 4, 64, 128)).reshape(16, 4, 64, 128), ("y", "x")
    ).reshape(BINS, 16, 64, 128)
    order = column_order(width)
    head_t = dot(order, head, 1, 1).astype(bf16)
    own_packed, head_t = lax.optimization_barrier((own_packed, head_t))
    other_packed = swap_core(own_packed)
    unpack = functools.partial(
        call, unpack_kernel, shape(BINS, hw, TOK, dtype=bf16), [VMEM], nbytes=4 * 2**20
    )
    own_cols = unpack(own_packed)
    own_cols, other_packed = lax.optimization_barrier((own_cols, other_packed))
    other_cols = unpack(other_packed)

    def pick(a, b):
        return lax.dynamic_index_in_dim(a, b, 0, keepdims=False)

    def partial_logits(r):
        return dot(pick(own_cols, at[r]), head_t[:hw], 0, 0) + dot(pick(other_cols, at[r]), head_t[hw:], 0, 0)

    far = partial_logits(2)
    far, own_cols, other_cols = lax.optimization_barrier((far, own_cols, other_cols))
    from_left = shift(far[:half], 1)
    from_right = shift(far[half:], 3)
    up = partial_logits(1)
    down = partial_logits(3)
    own = partial_logits(0)
    up, down = lax.optimization_barrier((up, down))
    nothing = jnp.zeros((half, vocab_rows), f32)
    up = shift(up + jnp.concatenate([from_left, nothing]), 1)
    down = shift(down + jnp.concatenate([nothing, from_right]), 3)

    mask_f = loss_mask[0].astype(f32)
    seg_ids = segments[0]
    same = (seg_ids[:, None] == seg_ids[None, :]).astype(f32)
    counts = jnp.sum(same * mask_f[None, :], axis=1)
    shard = ((lax.axis_index("zh") * 4 + lax.axis_index("zl")) * 4 + lax.axis_index("x")) * 2
    vocab_start = (shard + lax.axis_index("c")) * vocab_rows
    place = (targets[0] - vocab_start)[:, None]
    row = (64 * targets + loss_mask * counts.astype(i32)[None]).astype(f32)
    here = jnp.stack([lax.axis_index("x") * 2 + lax.axis_index("c"), vocab_start, y]).astype(i32)

    exps, lse, facts = call(
        softmax_kernel,
        [shape(TOK, vocab_rows, dtype=bf16), shape(16, 1, TOK), shape(3, TOK)],
        [VMEM] * 3,
        own + up + down,
        place,
        row,
    )
    exps, lse = lax.optimization_barrier((exps, lse))

    every_exp = [exps, shift(exps, 3), shift(exps, 2), shift(exps, 1)]
    facts = call(combine_kernel, shape(32, 4, TOK), [VMEM] * 2, exchange(lse, Z), facts, flops=3 * 10**10)
    facts = exchange(facts, ("y", "x", "c"))
    facts, every_exp = lax.optimization_barrier((facts, every_exp))

    grads, sent = call(
        grad_kernel,
        [shape(BINS, TOK, vocab_rows, dtype=bf16), shape(BINS, 16, 64, 128, dtype=bf16)],
        [SMEM] + [VMEM] * 5 + [FREE],
        here,
        facts,
        *every_exp,
        head_t,
    )
    terms = swap_core(sent)
    kept = call(kept_kernel, shape(BINS, 16, 64, 128), [FREE, VMEM], head_t, grads, flops=10**9)
    head_terms = call(
        head_kernel, shape(width, vocab_rows, dtype=bf16), [FREE, FREE, VMEM], own_cols, other_cols, grads, flops=2 * 10**9
    )
    terms, kept = lax.optimization_barrier((terms, kept))
    terms = (kept + terms.astype(f32)).astype(bf16).reshape(16, 4, 64, 128)
    terms = exchange(terms, ("y", "x")).reshape(BINS, 4, 4, 64, 128)
    terms = jnp.sum(terms.astype(f32), axis=1).astype(bf16).reshape(16, 64, 128)
    terms = exchange(terms, Z)
    grad_hidden = unpacked(jnp.sum(terms.astype(f32), axis=0)).astype(bf16).T
    grad_head = dot(head_terms, order, 0, 0).astype(bf16)
    return (grad_hidden, grad_head)


def solution(mesh):
    fine = Mesh(mesh.devices.reshape(4, 4, 4, 4, 2), EVERY)
    placed = (P("y", ROW), P(ROW, "y"), P("y", None), P("y", None), P("y", None))
    return jax.shard_map(
        body,
        mesh=fine,
        in_specs=placed,
        out_specs=(P("y", ROW), P(ROW, "y")),
        check_vma=False,
    )
```

```python
import functools

import jax
import jax.numpy as jnp
from jax import lax
from jax.experimental import pallas as pl
from jax.experimental.pallas import tpu as pltpu
from jax.sharding import Mesh
from jax.sharding import PartitionSpec as P

loss_scale = 256.0
BINS = 4
EVERY = ("y", "zh", "zl", "x", "c")
ROW = ("zh", "zl", "x", "c")
Z = ("zh", "zl")
COLS, TOK, HIGH, EXTRA = 40, 192, 64, 24
f32, bf16, i32 = jnp.float32, jnp.bfloat16, jnp.int32
VMEM = pl.BlockSpec(memory_space=pltpu.VMEM)
FREE = pl.BlockSpec()
SMEM = pl.BlockSpec(memory_space=pltpu.SMEM)


def shift(a, k):
    return lax.ppermute(a, "y", [(i, (i + k) % BINS) for i in range(BINS)])


def swap_core(a):
    return lax.ppermute(a, "c", [(0, 1), (1, 0)])


def exchange(a, axes):
    return lax.all_to_all(a, axes, 0, 0, tiled=True)


def call(kernel, out, ins, *args, flops=0, nbytes=0, scratch=()):
    return pl.pallas_call(
        kernel,
        out_shape=out,
        in_specs=ins,
        scratch_shapes=list(scratch),
        out_specs=[VMEM] * len(out) if isinstance(out, (list, tuple)) else VMEM,
        compiler_params=pltpu.CompilerParams(vmem_limit_bytes=16 * 2**20),
        cost_estimate=pl.CostEstimate(flops=flops, bytes_accessed=nbytes, transcendentals=0),
    )(*args)


def shape(*dims, dtype=f32):
    return jax.ShapeDtypeStruct(dims, dtype)


def packed(piece):
    tail = piece[:, 128:]
    right = jnp.concatenate([tail[EXTRA:], jnp.zeros((2 * EXTRA - COLS, TOK - 128), f32)], axis=0)
    return jnp.concatenate([piece[:, :128], jnp.concatenate([tail[:EXTRA], right], axis=1)], axis=0)


def unpacked(piece):
    tail = jnp.concatenate([piece[COLS:, :64], piece[COLS : 2 * COLS - EXTRA, 64:]], axis=0)
    return jnp.concatenate([piece[:COLS], tail], axis=1)


def pack_kernel(h_ref, o_ref):
    piece = packed(h_ref[...].astype(f32)).astype(bf16)
    for k in range(16):
        o_ref[k] = piece


def unpack_kernel(a_ref, o_ref):
    def one(b, _):
        for p in range(8):
            pair = [unpacked(a_ref[b, 2 * p + k].astype(f32)) for k in range(2)]
            o_ref[b, 2 * COLS * p : 2 * COLS * (p + 1), :] = jnp.concatenate(pair, axis=0).astype(bf16)
        return 0

    lax.fori_loop(0, BINS, one, 0)


def eye():
    return lax.broadcasted_iota(i32, (TOK, TOK), 0) == lax.broadcasted_iota(i32, (TOK, TOK), 1)


def softmax_kernel(logits_ref, place_ref, row_ref, exps_ref, lse_ref, facts_ref):
    logits = logits_ref[...]
    top = jnp.max(logits, axis=1, keepdims=True)
    shifted = jnp.exp(logits - top)
    total = jnp.sum(shifted, axis=1, keepdims=True)
    lse = top + jnp.log(total)
    places = lax.broadcasted_iota(i32, logits.shape, 1)
    at_target = jnp.sum(jnp.where(place_ref[...] == places, logits, 0.0), axis=1, keepdims=True)
    exps_ref[...] = (shifted * (1.0 / total)).astype(bf16)
    same = eye()
    lanes = [jnp.sum(jnp.where(same, v, 0.0), axis=0, keepdims=True) for v in (lse, at_target)]
    facts_ref[...] = jnp.concatenate(lanes + [row_ref[...]], axis=0)
    for k in range(16):
        lse_ref[k] = lanes[0]


def log_sum_exp(part):
    top = jnp.max(part, axis=0, keepdims=True)
    return top + jnp.log(jnp.sum(jnp.exp(part - top), axis=0, keepdims=True))


def combine_kernel(lse_ref, facts_ref, o_ref):
    total = log_sum_exp(jnp.concatenate([lse_ref[k] for k in range(16)], axis=0))
    rows = jnp.concatenate([total, facts_ref[...]], axis=0)
    for k in range(32):
        o_ref[k] = rows


def put_terms(columns, grads, ref, b):
    terms = lax.dot_general(columns, grads, (((1,), (1,)), ((), ())), preferred_element_type=f32)
    for p in range(16):
        ref[b, p] = packed(terms[COLS * p : COLS * (p + 1)]).astype(ref.dtype)


def grad_kernel(where_ref, facts_ref, exps0, exps1, exps2, exps3, head_ref, grads_ref, sent_ref):
    same = eye()

    def column(row):
        return jnp.sum(jnp.where(same, row, 0.0), axis=1, keepdims=True)

    half = head_ref.shape[0] // 2
    places = lax.broadcasted_iota(i32, exps0.shape, 1) + where_ref[1]
    for r, exps_ref in enumerate([exps0, exps1, exps2, exps3]):
        b = lax.rem(where_ref[2] + r, BINS)
        norm = log_sum_exp(jnp.concatenate([facts_ref[8 * b + k][0:1] for k in range(8)], axis=0))
        mine = facts_ref[8 * b + where_ref[0]]
        code = mine[3:4].astype(i32)
        counts = (code & 63).astype(f32)
        weight = jnp.where(counts > 0, loss_scale / jnp.maximum(counts, 1.0), 0.0)
        scale = column(weight * jnp.exp(mine[1:2] - norm))
        hit = column(weight * (jnp.exp(mine[2:3] - norm) - 1.0))
        target = column((code >> 6).astype(f32)).astype(i32)
        grads = jnp.where(target == places, hit, exps_ref[...].astype(f32) * scale).astype(bf16)
        grads_ref[b] = grads
        put_terms(head_ref[half:], grads, sent_ref, b)


def kept_kernel(head_ref, grads_ref, kept_ref):
    for b in range(BINS):
        put_terms(head_ref[: head_ref.shape[0] // 2], grads_ref[b], kept_ref, b)


def head_kernel(own_ref, other_ref, grads_ref, o_ref):
    half = own_ref.shape[1]
    for h, ref in enumerate([own_ref, other_ref]):
        total = sum(jnp.dot(ref[b], grads_ref[b], preferred_element_type=f32) for b in range(BINS))
        o_ref[h * half : (h + 1) * half, :] = total.astype(bf16)


def column_order(width):
    half = width // 2
    p = lax.broadcasted_iota(i32, (width, 1), 0)
    core = lax.rem(lax.axis_index("c") + p // half, 2)
    q = lax.rem(p, half)
    natural = lax.rem(q // COLS, 4) * (8 * COLS) + q // (4 * COLS) * (2 * COLS) + core * COLS + lax.rem(q, COLS)
    return (natural == lax.broadcasted_iota(i32, (1, width), 1)).astype(bf16)


def dot(a, b, ca, cb):
    return lax.dot_general(a, b, (((ca,), (cb,)), ((), ())), preferred_element_type=f32)


def body(hidden, head, targets, segments, loss_mask):
    vocab_rows, width = head.shape
    half, hw = TOK // 2, width // 2
    y = lax.axis_index("y")
    at = [lax.rem(y + r, BINS) for r in range(BINS)]

    spread = call(pack_kernel, shape(16, 64, 128, dtype=bf16), [VMEM], hidden.T)
    along_z = exchange(spread, Z).reshape(BINS, 1, 4, 64, 128)
    own_packed = exchange(
        jnp.broadcast_to(along_z, (BINS, 4, 4, 64, 128)).reshape(16, 4, 64, 128), ("y", "x")
    ).reshape(BINS, 16, 64, 128)
    order = column_order(width)
    head_t = dot(order, head, 1, 1).astype(bf16)
    own_packed, head_t = lax.optimization_barrier((own_packed, head_t))
    other_packed = swap_core(own_packed)
    unpack = functools.partial(
        call, unpack_kernel, shape(BINS, hw, TOK, dtype=bf16), [VMEM], nbytes=4 * 2**20
    )
    own_cols = unpack(own_packed)
    own_cols, other_packed = lax.optimization_barrier((own_cols, other_packed))
    other_cols = unpack(other_packed)

    def pick(a, b):
        return lax.dynamic_index_in_dim(a, b, 0, keepdims=False)

    def partial_logits(r):
        return dot(pick(own_cols, at[r]), head_t[:hw], 0, 0) + dot(pick(other_cols, at[r]), head_t[hw:], 0, 0)

    far = partial_logits(2)
    far, own_cols, other_cols = lax.optimization_barrier((far, own_cols, other_cols))
    from_left = shift(far[:half], 1)
    from_right = shift(far[half:], 3)
    up = partial_logits(1)
    down = partial_logits(3)
    own = partial_logits(0)
    up, down = lax.optimization_barrier((up, down))
    nothing = jnp.zeros((half, vocab_rows), f32)
    up = shift(up + jnp.concatenate([from_left, nothing]), 1)
    down = shift(down + jnp.concatenate([nothing, from_right]), 3)

    mask_f = loss_mask[0].astype(f32)
    seg_ids = segments[0]
    same = (seg_ids[:, None] == seg_ids[None, :]).astype(f32)
    counts = jnp.sum(same * mask_f[None, :], axis=1)
    shard = ((lax.axis_index("zh") * 4 + lax.axis_index("zl")) * 4 + lax.axis_index("x")) * 2
    vocab_start = (shard + lax.axis_index("c")) * vocab_rows
    place = (targets[0] - vocab_start)[:, None]
    row = (64 * targets + loss_mask * counts.astype(i32)[None]).astype(f32)
    here = jnp.stack([lax.axis_index("x") * 2 + lax.axis_index("c"), vocab_start, y]).astype(i32)

    exps, lse, facts = call(
        softmax_kernel,
        [shape(TOK, vocab_rows, dtype=bf16), shape(16, 1, TOK), shape(3, TOK)],
        [VMEM] * 3,
        own + up + down,
        place,
        row,
    )
    exps, lse = lax.optimization_barrier((exps, lse))

    every_exp = [exps, shift(exps, 3), shift(exps, 2), shift(exps, 1)]
    facts = call(combine_kernel, shape(32, 4, TOK), [VMEM] * 2, exchange(lse, Z), facts, flops=3 * 10**10)
    facts = exchange(facts, ("y", "x", "c"))
    facts, every_exp = lax.optimization_barrier((facts, every_exp))

    grads, sent = call(
        grad_kernel,
        [shape(BINS, TOK, vocab_rows, dtype=bf16), shape(BINS, 16, 64, 128, dtype=bf16)],
        [SMEM] + [VMEM] * 5 + [FREE],
        here,
        facts,
        *every_exp,
        head_t,
    )
    terms = swap_core(sent)
    kept = call(kept_kernel, shape(BINS, 16, 64, 128), [FREE, VMEM], head_t, grads, flops=10**9)
    head_terms = call(
        head_kernel, shape(width, vocab_rows, dtype=bf16), [FREE, FREE, FREE], own_cols, other_cols, grads, flops=2 * 10**9
    )
    terms, kept = lax.optimization_barrier((terms, kept))
    terms = (kept + terms.astype(f32)).astype(bf16).reshape(16, 4, 64, 128)
    terms = exchange(terms, ("y", "x")).reshape(BINS, 4, 4, 64, 128)
    terms = jnp.sum(terms.astype(f32), axis=1).astype(bf16).reshape(16, 64, 128)
    terms = exchange(terms, Z)
    grad_hidden = unpacked(jnp.sum(terms.astype(f32), axis=0)).astype(bf16).T
    grad_head = dot(head_terms, order, 0, 0).astype(bf16)
    return (grad_hidden, grad_head)


def solution(mesh):
    fine = Mesh(mesh.devices.reshape(4, 4, 4, 4, 2), EVERY)
    placed = (P("y", ROW), P(ROW, "y"), P("y", None), P("y", None), P("y", None))
    return jax.shard_map(
        body,
        mesh=fine,
        in_specs=placed,
        out_specs=(P("y", ROW), P(ROW, "y")),
        check_vma=False,
    )
```
